1024 devices in a mesh: dp: 128 (over x_lo, z, y), mp: 8 (over x_hi, core).
Axes of the slice: x: 8 (x_hi: 4, x_lo: 2; x = x_hi * 2 + x_lo), y: 8, z: 8, core: 2. Of those that a mesh axis runs over, the one named last changes fastest.
Arguments:
- activations: bfloat16 [2, 14336, 8192], P(None, 'dp'), may hold values from -24 to 24
- cotangent: bfloat16 [2, 14336, 28672], P(None, 'dp', 'mp'), may hold values from -0.09375 to 0.09375
- subspace_basis: bfloat16 [28672, 512], P('mp'), may hold values from -0.046875 to 0.046875
- weight: bfloat16 [8192, 28672], P('dp', 'mp'), may hold values from -0.0625 to 0.0625
- moment: float32 [8192, 512], P('dp', 'mp'), may hold values from -2 to 2
- second: float32 [8192, 512], P('dp', 'mp'), may hold values from 0.25 to 4
Outputs:
- weight_new: bfloat16 [8192, 28672], P('dp', 'mp')
- moment_new: float32 [8192, 512], P('dp', 'mp')
- second_new: float32 [8192, 512], P('dp', 'mp')
The draws below stay inside these ranges and needn't reach their ends.
All inputs are finite; a program needn't handle non-finite values.
Results may differ from the reference program's by a relative error of at most 0.006.
Values may be sent and summed in bfloat16 or wider, within the bound.
A program may use at most 32 MiB of HBM per device.

```python
import math
import jax
import jax.numpy as jnp

D = 8192
FF = 28672
R = 512
MICRO = 2
TOKENS = 14336


def with_spikes(drawn, own_key, source, target, parts, factor):
    owner, partner = [(jnp.arange(drawn.shape[dim]) // (drawn.shape[dim] // parts)).reshape([-1 if axis == dim else 1 for axis in range(drawn.ndim)]) for dim in (source, target)]
    chosen = jax.random.permutation(own_key, parts)[partner]
    strong = (owner == chosen) | (owner == (partner + parts // 2) % parts)
    return jnp.where(strong, factor * drawn, drawn)


def steps_of(key, dims, split, low, high):
    level = 1.0
    for dim, blocks in split:
        steps = jax.random.uniform(jax.random.fold_in(jax.random.fold_in(key, 6), dim), (blocks,), jnp.float32, low / len(split), high / len(split))
        level = level * jnp.repeat(jnp.exp(steps), dims[dim] // blocks).reshape((-1,) + (1,) * (len(dims) - 1 - dim))
    return level


def gaussian(key, shape, spread, limit, split=(), kind=jnp.bfloat16):
    drawn = jax.random.normal(key, shape, jnp.float32) * spread
    if len(split) > 0:
        drawn = steps_of(key, shape, split, -0.22, 0.18) * drawn
    return jnp.clip(drawn, min=-limit, max=limit).astype(kind)


def heavy_noise(own_key, dims, spread, bound, split, heavy, held_as=jnp.bfloat16):
    array = spread * jax.random.normal(own_key, dims, jnp.float32)
    if split:
        array = array * steps_of(own_key, dims, split, -0.22, 0.18)
    return jnp.clip(with_spikes(array, jax.random.fold_in(own_key, 3), *heavy), -bound, bound).astype(held_as)


def setup_inputs(seed: int = 0) -> dict:
    key_list = jax.random.split(jax.random.key(seed), 7)
    activations = heavy_noise(key_list[0], (MICRO, TOKENS, D), 1.0, 24.0, ((1, 128),), (1, 2, 128, 5.5))
    cotangent = gaussian(key_list[1], (MICRO, TOKENS, FF), ((MICRO * TOKENS) ** -0.5), 0.09375, ((1, 128), (2, 8)))
    subspace_basis = heavy_noise(key_list[2], (FF, R), FF ** -0.5, 0.046875, ((0, 8),), (0, 1, 8, 2.0))
    weight = gaussian(key_list[3], (D, FF), D ** -0.5, 0.0625, ((0, 128), (1, 8)))
    moment = gaussian(key_list[4], (D, R), 0.15, 2.0, ((0, 128), (1, 8)), jnp.float32)
    second = jnp.clip(jnp.exp(math.log(4.0) - 2.7725887 * jax.random.uniform(key_list[5], (D, R), jnp.float32) ** steps_of(key_list[5], (D, R), ((0, 128), (1, 8)), -0.2, 0.2)), 0.25, 4.0)
    return dict(activations=activations, cotangent=cotangent, subspace_basis=subspace_basis, weight=weight, moment=moment, second=second)


beta_first = 0.9
beta_second = 0.999
epsilon = 1e-08
step_size = 0.25

def reference(activations, cotangent, subspace_basis, weight, moment, second):
    gradient = jnp.zeros((D, R), jnp.float32)
    for number in range(MICRO):
        projected = jnp.dot(cotangent[number], subspace_basis, preferred_element_type=jnp.float32).astype(jnp.bfloat16)
        gradient = gradient + jnp.dot(activations[number].T, projected, preferred_element_type=jnp.float32)
    moment_new = beta_first * moment + (1.0 - beta_first) * gradient
    second_new = beta_second * second + (1.0 - beta_second) * gradient * gradient
    direction = (moment_new / (jnp.sqrt(second_new) + epsilon)).astype(jnp.bfloat16)
    update = jnp.dot(direction, subspace_basis.T, preferred_element_type=jnp.float32)
    weight_new = (weight.astype(jnp.float32) - step_size * update).astype(jnp.bfloat16)
    return (weight_new, moment_new, second_new)
```

```python
import functools
import math

import jax
import jax.numpy as jnp
from jax import lax
from jax.experimental import pallas as pl
from jax.experimental.pallas import tpu as pltpu
from jax.sharding import PartitionSpec as P

beta_first = 0.9
beta_second = 0.999
epsilon = 1e-08
step_size = 0.25

F32 = jnp.float32
BF16 = jnp.bfloat16
MESH_ID = pl.DeviceIdType.MESH
OWN = 64
HALF = 16
DEPTH = 512


def halves(top, bottom, low):
    first = jnp.where(low, top, pltpu.roll(bottom, 64, 1))
    second = jnp.where(low, pltpu.roll(top, 64, 1), bottom)
    return first, second


def kernel(
    side, n_mp, act_hbm, cot_hbm, basis_hbm, weight_hbm, moment_hbm, second_hbm,
    weight_out, moment_out, second_out,
    act, cot, basis, weight, moment, second, new_weight, new_moment, new_second,
    partial, mp_send, mp_recv, rows_t, y_send, z_send, y_recv, z_recv,
    zz_send, yy_send, zz_recv, yy_recv, x_send, x_recv, gather,
    load_sem, part_sem, store_sem, mp_ss, mp_rs, y_ss, y_rs, z_ss, z_rs,
    zz_ss, zz_rs, yy_ss, yy_rs, x_ss, x_rs, g_ss, g_rs,
):
    dp = lax.axis_index("dp")
    mp = lax.axis_index("mp")
    y = lax.rem(dp, side)
    z = lax.rem(dp // side, side)
    x = dp // (side * side)

    def y_peer(k):
        return (dp - y + lax.rem(y + k, side), mp)

    def z_peer(k):
        return (dp + (lax.rem(z + k, side) - z) * side, mp)

    def mp_peer(k):
        return (dp, lax.rem(mp + k, n_mp))

    x_peer = (dp + (1 - 2 * x) * side * side, mp)

    def remote(src, dst, send_sem, recv_sem, device):
        return pltpu.make_async_remote_copy(
            src_ref=src, dst_ref=dst, send_sem=send_sem, recv_sem=recv_sem,
            device_id=device, device_id_type=MESH_ID,
        )

    tokens = act.shape[0]
    micro = tokens // 2
    depth_all = basis.shape[0]
    parts = depth_all // DEPTH

    def part_copies(i):
        span = pl.ds(i * DEPTH, DEPTH)
        return (
            pltpu.make_async_copy(basis_hbm.at[span, :], basis.at[span, :], part_sem.at[0, i]),
            pltpu.make_async_copy(cot_hbm.at[:, span], cot.at[:, span], part_sem.at[1, i]),
        )

    for i in range(parts):
        for copy in part_copies(i):
            copy.start()
    loads = [
        pltpu.make_async_copy(act_hbm, act, load_sem.at[0]),
        pltpu.make_async_copy(moment_hbm, moment, load_sem.at[1]),
        pltpu.make_async_copy(second_hbm, second, load_sem.at[2]),
        pltpu.make_async_copy(weight_hbm, weight, load_sem.at[3]),
    ]
    for copy in loads:
        copy.start()

    barrier = pltpu.get_barrier_semaphore()
    for k in range(1, n_mp):
        pl.semaphore_signal(barrier, inc=1, device_id=mp_peer(k), device_id_type=MESH_ID)
    for k in range(1, side):
        pl.semaphore_signal(barrier, inc=1, device_id=y_peer(k), device_id_type=MESH_ID)
        pl.semaphore_signal(barrier, inc=1, device_id=z_peer(k), device_id_type=MESH_ID)
    pl.semaphore_signal(barrier, inc=1, device_id=x_peer, device_id_type=MESH_ID)

    for i in range(parts):
        for copy in part_copies(i):
            copy.wait()
        span = slice(i * DEPTH, (i + 1) * DEPTH)
        term = jnp.dot(cot[:, span], basis[span, :], preferred_element_type=F32)
        if i == 0:
            partial[...] = term
        else:
            partial[...] += term

    low_micro = lax.broadcasted_iota(jnp.int32, (micro, 128), 1) < 64
    for t in range(n_mp // 2):
        cols = slice(t * 128, (t + 1) * 128)
        first, second_tile = halves(partial[:micro, cols], partial[micro:, cols], low_micro)
        mp_send[2 * t] = first.astype(BF16)
        mp_send[2 * t + 1] = second_tile.astype(BF16)

    pl.semaphore_wait(barrier, n_mp - 1 + 2 * (side - 1) + 1)

    def mp_copy(k):
        return remote(
            mp_send.at[lax.rem(mp + k, n_mp)], mp_recv.at[k - 1], mp_ss.at[k - 1], mp_rs.at[k - 1], mp_peer(k)
        )

    for k in range(1, n_mp):
        mp_copy(k).start()
    total = mp_send[mp].astype(F32)
    for k in range(1, n_mp):
        mp_copy(k).wait_recv()
        total = total + mp_recv[k - 1].astype(F32)
    projected = total.astype(BF16).astype(F32)
    stacked = jnp.concatenate(
        [projected, pltpu.roll(projected, 64, 1), jnp.zeros((256 - tokens, 128), F32)], axis=0
    )
    rows_t[...] = stacked.T[:OWN, :].astype(BF16)

    loads[0].wait()
    lhs = rows_t[:, :tokens]
    low = lax.broadcasted_iota(jnp.int32, (32, 128), 1) < 64

    def z_copy(k):
        return remote(
            z_send.at[lax.rem(z + k, side)], z_recv.at[k - 1], z_ss.at[k - 1], z_rs.at[k - 1], z_peer(k)
        )

    def y_copy(k):
        return remote(
            y_send.at[lax.rem(y + k, side)], y_recv.at[k - 1], y_ss.at[k - 1], y_rs.at[k - 1], y_peer(k)
        )

    width = side * OWN

    def gradient_of(k, carry):
        to_z = lax.rem(z + k, side)
        for to_x in range(2):
            start = pl.multiple_of((to_x * side + to_z) * width, 128)
            grad = jnp.dot(lhs, act[:, pl.ds(start, width)], preferred_element_type=F32)
            for pair in range(side // 2):
                tile = grad[:, pair * 128 : (pair + 1) * 128]
                for lo, block in enumerate(halves(tile[:32], tile[32:], low)):
                    block = block.astype(BF16)
                    y_send[2 * pair + lo, to_x, to_z] = block[:HALF]
                    z_send[to_z, to_x, 2 * pair + lo] = block[HALF:]

        @pl.when(k < side)
        def _():
            z_copy(k).start()

        return carry

    lax.fori_loop(1, side + 1, gradient_of, 0)
    for k in range(1, side):
        y_copy(k).start()

    def add_first(copy, send, recv, own, out):
        for k in range(1, side):
            copy(k).wait_recv()

        def body(q, carry):
            for to_x in range(2):
                acc = send[own, to_x, q].astype(F32)
                for k in range(side - 1):
                    acc = acc + recv[k, to_x, q].astype(F32)
                out[q, to_x] = acc.astype(BF16)
            return carry

        lax.fori_loop(0, side, body, 0)

    def yy_copy(k):
        return remote(
            yy_send.at[lax.rem(y + k, side)], yy_recv.at[k - 1], yy_ss.at[k - 1], yy_rs.at[k - 1], y_peer(k)
        )

    def zz_copy(k):
        return remote(
            zz_send.at[lax.rem(z + k, side)], zz_recv.at[k - 1], zz_ss.at[k - 1], zz_rs.at[k - 1], z_peer(k)
        )

    add_first(z_copy, z_send, z_recv, z, yy_send)
    for k in range(1, side):
        yy_copy(k).start()
    add_first(y_copy, y_send, y_recv, y, zz_send)
    for k in range(1, side):
        zz_copy(k).start()

    def add_second(copy, send, recv, own, half):
        acc = [send[own, to_x].astype(F32) for to_x in range(2)]
        for k in range(1, side):
            copy(k).wait_recv()
            for to_x in range(2):
                acc[to_x] = acc[to_x] + recv[k - 1, to_x].astype(F32)
        for to_x in range(2):
            x_send[to_x, half * HALF : (half + 1) * HALF, :] = acc[to_x]

    add_second(yy_copy, yy_send, yy_recv, y, 1)
    add_second(zz_copy, zz_send, zz_recv, z, 0)
    x_copy = remote(x_send.at[1 - x], x_recv, x_ss, x_rs, x_peer)
    x_copy.start()
    x_copy.wait_recv()
    packed = x_send[x] + x_recv[...]
    grad_t = jnp.concatenate([packed, pltpu.roll(packed, 64, 1)], axis=0)
    grad = grad_t.T[:OWN, :]

    loads[1].wait()
    loads[2].wait()
    moment_new = beta_first * moment[...] + (1.0 - beta_first) * grad
    second_new = beta_second * second[...] + (1.0 - beta_second) * grad * grad
    new_moment[...] = moment_new
    new_second[...] = second_new
    direction = moment_new / (jnp.sqrt(second_new) + epsilon)
    twice = jnp.concatenate([direction, direction], axis=1)
    mine = lax.broadcasted_iota(jnp.int32, (OWN, 128), 1) // 64 == lax.rem(mp, 2)
    gather[mp] = jnp.where(mine, twice, 0.0).astype(BF16)

    def g_copy(k):
        return remote(gather.at[mp], gather.at[mp], g_ss.at[k - 1], g_rs.at[k - 1], mp_peer(k))

    def g_arrival(k):
        slot = lax.rem(mp + n_mp - k, n_mp)
        return remote(gather.at[slot], gather.at[slot], g_ss.at[k - 1], g_rs.at[k - 1], mp_peer(k))

    for k in range(1, n_mp):
        g_copy(k).start()
    stores = [
        pltpu.make_async_copy(new_moment, moment_out, store_sem.at[0]),
        pltpu.make_async_copy(new_second, second_out, store_sem.at[1]),
    ]
    for copy in stores:
        copy.start()
    loads[3].wait()
    for k in range(1, n_mp):
        g_arrival(k).wait_recv()
    left = jnp.concatenate([gather[2 * t] + gather[2 * t + 1] for t in range(n_mp // 2)], axis=1)

    for i in range(parts):
        span = slice(i * DEPTH, (i + 1) * DEPTH)
        update = lax.dot_general(left, basis[span, :], (((1,), (1,)), ((), ())), preferred_element_type=F32)
        new_weight[:, span] = (weight[:, span].astype(F32) - step_size * update).astype(BF16)
    stores.append(pltpu.make_async_copy(new_weight, weight_out, store_sem.at[2]))
    stores[-1].start()

    for k in range(1, n_mp):
        mp_copy(k).wait_send()
        g_copy(k).wait_send()
    for k in range(1, side):
        z_copy(k).wait_send()
        y_copy(k).wait_send()
        yy_copy(k).wait_send()
        zz_copy(k).wait_send()
    x_copy.wait_send()
    for copy in stores:
        copy.wait()


def shards(side, n_mp, activations, cotangent, subspace_basis, weight, moment, second):
    micro, tokens, width = activations.shape
    act = activations.reshape(micro * tokens, width)
    cot = cotangent.reshape(micro * tokens, cotangent.shape[2])
    units, rank = subspace_basis.shape
    dma = pltpu.SemaphoreType.DMA
    n = side - 1
    m = n_mp - 1
    block = (2, HALF, 128)
    plane = (2, side, HALF, 128)
    scratch = [
        pltpu.VMEM(act.shape, BF16),
        pltpu.VMEM(cot.shape, BF16),
        pltpu.VMEM(subspace_basis.shape, BF16),
        pltpu.VMEM(weight.shape, BF16),
        pltpu.VMEM(moment.shape, F32),
        pltpu.VMEM(second.shape, F32),
        pltpu.VMEM(weight.shape, BF16),
        pltpu.VMEM(moment.shape, F32),
        pltpu.VMEM(second.shape, F32),
        pltpu.VMEM((micro * tokens, rank), F32),
        pltpu.VMEM((n_mp, tokens, 128), BF16),
        pltpu.VMEM((m, tokens, 128), BF16),
        pltpu.VMEM((OWN, 256), BF16),
        pltpu.VMEM((side,) + plane, BF16),
        pltpu.VMEM((side,) + plane, BF16),
        pltpu.VMEM((n,) + plane, BF16),
        pltpu.VMEM((n,) + plane, BF16),
        pltpu.VMEM((side,) + block, BF16),
        pltpu.VMEM((side,) + block, BF16),
        pltpu.VMEM((n,) + block, BF16),
        pltpu.VMEM((n,) + block, BF16),
        pltpu.VMEM((2, 32, 128), F32),
        pltpu.VMEM((32, 128), F32),
        pltpu.VMEM((n_mp, OWN, 128), BF16),
        dma((4,)),
        dma((2, units // DEPTH)),
        dma((3,)),
        dma((m,)), dma((m,)),
        dma((n,)), dma((n,)), dma((n,)), dma((n,)),
        dma((n,)), dma((n,)), dma((n,)), dma((n,)),
        dma(()), dma(()),
        dma((m,)), dma((m,)),
    ]
    hbm = pl.BlockSpec(memory_space=pltpu.HBM)
    rows, owned_units = weight.shape
    return pl.pallas_call(
        functools.partial(kernel, side, n_mp),
        out_shape=(
            jax.ShapeDtypeStruct(weight.shape, BF16),
            jax.ShapeDtypeStruct(moment.shape, F32),
            jax.ShapeDtypeStruct(second.shape, F32),
        ),
        in_specs=[hbm] * 6,
        out_specs=(hbm,) * 3,
        scratch_shapes=scratch,
        compiler_params=pltpu.CompilerParams(
            collective_id=0, has_side_effects=True, vmem_limit_bytes=60 * 1024 * 1024
        ),
    )(act, cot, subspace_basis, weight, moment, second)


def solution(mesh):
    side = math.isqrt(mesh.shape["dp"] // 2)
    n_mp = mesh.shape["mp"]
    in_specs = (
        P(None, "dp", None),
        P(None, "dp", "mp"),
        P("mp", None),
        P("dp", "mp"),
        P("dp", "mp"),
        P("dp", "mp"),
    )
    out_specs = (P("dp", "mp"), P("dp", "mp"), P("dp", "mp"))
    return jax.shard_map(
        functools.partial(shards, side, n_mp), mesh=mesh, in_specs=in_specs, out_specs=out_specs, check_vma=False
    )
```

```python
import functools
import math

import jax
import jax.numpy as jnp
from jax import lax
from jax.experimental import pallas as pl
from jax.experimental.pallas import tpu as pltpu
from jax.sharding import PartitionSpec as P

beta_first = 0.9
beta_second = 0.999
epsilon = 1e-08
step_size = 0.25

F32 = jnp.float32
BF16 = jnp.bfloat16
MESH_ID = pl.DeviceIdType.MESH
OWN = 64
HALF = 16
DEPTH = 512


def halves(top, bottom, low):
    first = jnp.where(low, top, pltpu.roll(bottom, 64, 1))
    second = jnp.where(low, pltpu.roll(top, 64, 1), bottom)
    return first, second


def low_lanes(rows):
    return lax.broadcasted_iota(jnp.int32, (rows, 128), 1) < 64


def gradient_kernel(
    side, n_mp, act_hbm, cot_hbm, basis_hbm, moment_hbm, second_hbm,
    gather_out, grad_out,
    act, cot, basis, moment, second, grad_own,
    partial, mp_send, mp_recv, rows_t, y_send, z_send,
    y_recv1, y_recv2, y_recv3, y_recv4, z_recv1, z_recv2, z_recv3, z_recv4,
    zz_send, yy_send, zz_recv, yy_recv, x_send, x_recv, gather,
    load_sem, part_sem, store_sem, mp_ss, mp_rs, y_ss, y_rs, z_ss, z_rs,
    zz_ss, zz_rs, yy_ss, yy_rs, x_ss, x_rs, g_ss, g_rs,
):
    dp = lax.axis_index("dp")
    mp = lax.axis_index("mp")
    y = lax.rem(dp, side)
    z = lax.rem(dp // side, side)
    x = dp // (side * side)

    def y_peer(k):
        return (dp - y + lax.rem(y + k, side), mp)

    def z_peer(k):
        return (dp + (lax.rem(z + k, side) - z) * side, mp)

    def mp_peer(k):
        return (dp, lax.rem(mp + k, n_mp))

    x_peer = (dp + (1 - 2 * x) * side * side, mp)

    def remote(src, dst, send_sem, recv_sem, device):
        return pltpu.make_async_remote_copy(
            src_ref=src, dst_ref=dst, send_sem=send_sem, recv_sem=recv_sem,
            device_id=device, device_id_type=MESH_ID,
        )

    tokens = act.shape[0]
    micro = tokens // 2
    parts = basis.shape[0] // DEPTH

    def part_copies(i):
        span = pl.ds(i * DEPTH, DEPTH)
        return (
            pltpu.make_async_copy(basis_hbm.at[span, :], basis.at[span, :], part_sem.at[0, i]),
            pltpu.make_async_copy(cot_hbm.at[:, span], cot.at[:, span], part_sem.at[1, i]),
        )

    for i in range(parts):
        for copy in part_copies(i):
            copy.start()
    loads = [
        pltpu.make_async_copy(act_hbm, act, load_sem.at[0]),
        pltpu.make_async_copy(moment_hbm, moment, load_sem.at[1]),
        pltpu.make_async_copy(second_hbm, second, load_sem.at[2]),
    ]
    for copy in loads:
        copy.start()

    barrier = pltpu.get_barrier_semaphore()
    for k in range(1, n_mp):
        pl.semaphore_signal(barrier, inc=1, device_id=mp_peer(k), device_id_type=MESH_ID)
    for k in range(1, side):
        pl.semaphore_signal(barrier, inc=1, device_id=y_peer(k), device_id_type=MESH_ID)
        pl.semaphore_signal(barrier, inc=1, device_id=z_peer(k), device_id_type=MESH_ID)
    pl.semaphore_signal(barrier, inc=1, device_id=x_peer, device_id_type=MESH_ID)

    for i in range(parts):
        for copy in part_copies(i):
            copy.wait()
        span = slice(i * DEPTH, (i + 1) * DEPTH)
        term = jnp.dot(cot[:, span], basis[span, :], preferred_element_type=F32)
        if i == 0:
            partial[...] = term
        else:
            partial[...] += term

    for t in range(n_mp // 2):
        cols = slice(t * 128, (t + 1) * 128)
        first, other = halves(partial[:micro, cols], partial[micro:, cols], low_lanes(micro))
        mp_send[2 * t] = first.astype(BF16)
        mp_send[2 * t + 1] = other.astype(BF16)

    pl.semaphore_wait(barrier, n_mp - 1 + 2 * (side - 1) + 1)

    def mp_copy(k):
        return remote(
            mp_send.at[lax.rem(mp + k, n_mp)], mp_recv.at[k - 1], mp_ss.at[k - 1], mp_rs.at[k - 1], mp_peer(k)
        )

    for k in range(1, n_mp):
        mp_copy(k).start()
    total = mp_send[mp].astype(F32)
    for k in range(1, n_mp):
        mp_copy(k).wait_recv()
        total = total + mp_recv[k - 1].astype(F32)
    projected = total.astype(BF16).astype(F32)
    stacked = jnp.concatenate(
        [projected, pltpu.roll(projected, 64, 1), jnp.zeros((256 - tokens, 128), F32)], axis=0
    )
    rows_t[...] = stacked.T[:OWN, :].astype(BF16)

    loads[0].wait()
    y_lhs = rows_t[:32, :tokens]
    z_lhs = rows_t[32:, :tokens]
    width = side * OWN

    def z_blocks(offset):
        to_z = lax.rem(z + offset, side)
        for to_x in range(2):
            start = pl.multiple_of((to_x * side + to_z) * width, 128)
            grad = jnp.dot(z_lhs, act[:, pl.ds(start, width)], preferred_element_type=F32)
            for pair in range(side // 2):
                tile = grad[:, pair * 128 : (pair + 1) * 128]
                for lo, block in enumerate(halves(tile[:HALF], tile[HALF:], low_lanes(HALF))):
                    z_send[to_z, to_x, 2 * pair + lo] = block.astype(BF16)

    def y_blocks(offset):
        pair = lax.rem(y // 2 + offset, side // 2)
        for to_x in range(2):
            for q in range(side // 2):
                tiles = []
                for to_z in (2 * q, 2 * q + 1):
                    start = pl.multiple_of((to_x * side + to_z) * width + pair * 128, 128)
                    tiles.append(act[:, pl.ds(start, 128)])
                grad = jnp.dot(y_lhs, jnp.concatenate(tiles, axis=1), preferred_element_type=F32)
                for r in range(2):
                    tile = grad[:, r * 128 : (r + 1) * 128]
                    for lo, block in enumerate(halves(tile[:HALF], tile[HALF:], low_lanes(HALF))):
                        y_send[2 * pair + lo, to_x, 2 * q + r] = block.astype(BF16)

    def axis(pos, peer, send, recv1, recv2, recv3, recv4, ss, rs):
        def block(offset):
            return send.at[lax.rem(pos + offset, side)]

        up, down = (1, 2, 3), (side - 1, side - 2, side - 3)
        near, merged, far, across = [], [], [], []
        for way, (one, two, three) in enumerate((up, down)):
            near.append(remote(block(one), recv1.at[way], ss.at[0, way], rs.at[0, way], peer(one)))
            merged.append(remote(block(two), recv2.at[way], ss.at[1, way], rs.at[1, way], peer(two)))
            far.append(remote(block(three), recv3.at[way], ss.at[2, way], rs.at[2, way], peer(one)))
            across.append(remote(block(4).at[way], recv4.at[way], ss.at[3, way], rs.at[3, way], peer(two)))

        def merge():
            for way, two in enumerate((2, side - 2)):
                slot = lax.rem(pos + two, side)
                far[way].wait_recv()
                across[way].wait_recv()
                for to_x in range(2):
                    acc = send[slot, to_x].astype(F32) + recv3[way, to_x].astype(F32)
                    if to_x == way:
                        acc = acc + recv4[way].astype(F32)
                    send[slot, to_x] = acc.astype(BF16)
                merged[way].start()

        def total(out):
            for way in range(2):
                near[way].wait_recv()
                merged[way].wait_recv()
            for to_x in range(2):
                acc = send[pos, to_x].astype(F32)
                for recv in (recv1, recv2):
                    for way in range(2):
                        acc = acc + recv[way, to_x].astype(F32)
                acc = acc.astype(BF16)
                for q in range(side):
                    out[q, to_x] = acc[q]

        return near, merged, far, across, merge, total

    z_near, z_merged, z_far, z_across, z_merge, z_total = axis(
        z, z_peer, z_send, z_recv1, z_recv2, z_recv3, z_recv4, z_ss, z_rs
    )
    y_near, y_merged, y_far, y_across, y_merge, y_total = axis(
        y, y_peer, y_send, y_recv1, y_recv2, y_recv3, y_recv4, y_ss, y_rs
    )

    def begin(copies):
        for copy in copies:
            copy.start()

    z_blocks(4)
    begin(z_across)
    z_blocks(3)
    z_blocks(side - 3)
    begin(z_far)
    y_blocks(2)
    begin(y_across)
    y_blocks(1)
    y_blocks(3)
    begin(y_far)
    z_blocks(1)
    z_blocks(side - 1)
    begin(z_near)
    y_blocks(0)
    begin(y_near)
    z_blocks(2)
    z_blocks(side - 2)
    z_merge()
    y_merge()
    z_blocks(0)

    def yy_copy(k):
        return remote(
            yy_send.at[lax.rem(y + k, side)], yy_recv.at[k - 1], yy_ss.at[k - 1], yy_rs.at[k - 1], y_peer(k)
        )

    def zz_copy(k):
        return remote(
            zz_send.at[lax.rem(z + k, side)], zz_recv.at[k - 1], zz_ss.at[k - 1], zz_rs.at[k - 1], z_peer(k)
        )

    z_total(yy_send)
    for k in range(1, side):
        yy_copy(k).start()
    y_total(zz_send)
    for k in range(1, side):
        zz_copy(k).start()

    def add_second(copy, send, recv, own, half):
        acc = [send[own, to_x].astype(F32) for to_x in range(2)]
        for k in range(1, side):
            copy(k).wait_recv()
            for to_x in range(2):
                acc[to_x] = acc[to_x] + recv[k - 1, to_x].astype(F32)
        for to_x in range(2):
            x_send[to_x, half * HALF : (half + 1) * HALF, :] = acc[to_x]

    add_second(yy_copy, yy_send, yy_recv, y, 1)
    add_second(zz_copy, zz_send, zz_recv, z, 0)
    x_copy = remote(x_send.at[1 - x], x_recv, x_ss, x_rs, x_peer)
    x_copy.start()
    x_copy.wait_recv()
    packed = x_send[x] + x_recv[...]
    rolled = pltpu.roll(packed, 64, 1)
    grad_t = jnp.concatenate([packed[:HALF], rolled[:HALF], packed[HALF:], rolled[HALF:]], axis=0)
    grad = grad_t.T[:OWN, :]

    loads[1].wait()
    loads[2].wait()
    moment_new = beta_first * moment[...] + (1.0 - beta_first) * grad
    second_new = beta_second * second[...] + (1.0 - beta_second) * grad * grad
    direction = moment_new / (jnp.sqrt(second_new) + epsilon)
    gather[mp] = jnp.concatenate([direction[:32], direction[32:]], axis=1).astype(BF16)

    def g_copy(k):
        return remote(gather.at[mp], gather.at[mp], g_ss.at[k - 1], g_rs.at[k - 1], mp_peer(k))

    def g_arrival(k):
        slot = lax.rem(mp + n_mp - k, n_mp)
        return remote(gather.at[slot], gather.at[slot], g_ss.at[k - 1], g_rs.at[k - 1], mp_peer(k))

    for k in range(1, n_mp):
        g_copy(k).start()
    grad_own[...] = grad
    grad_store = pltpu.make_async_copy(grad_own, grad_out, store_sem.at[0])
    grad_store.start()
    for k in range(1, n_mp):
        mp_copy(k).wait_send()
    for copies in (z_near, z_merged, z_far, z_across, y_near, y_merged, y_far, y_across):
        for copy in copies:
            copy.wait_send()
    for k in range(1, side):
        yy_copy(k).wait_send()
        zz_copy(k).wait_send()
    x_copy.wait_send()
    for k in range(1, n_mp):
        g_arrival(k).wait_recv()
    gather_store = pltpu.make_async_copy(gather, gather_out, store_sem.at[1])
    gather_store.start()
    for k in range(1, n_mp):
        g_copy(k).wait_send()
    grad_store.wait()
    gather_store.wait()


def weight_kernel(
    n_mp, gather_hbm, grad_hbm, basis_hbm, weight_hbm, moment_hbm, second_hbm,
    weight_out, moment_out, second_out,
    gather, grad, basis, weight, moment, second, new_weight, new_moment, new_second, load_sem, part_sem, store_sem,
):
    parts = basis.shape[0] // DEPTH

    def part_copy(i):
        span = pl.ds(i * DEPTH, DEPTH)
        return pltpu.make_async_copy(basis_hbm.at[span, :], basis.at[span, :], part_sem.at[0, i])

    def out_copy(i):
        span = pl.ds(i * DEPTH, DEPTH)
        return pltpu.make_async_copy(new_weight.at[:, span], weight_out.at[:, span], part_sem.at[1, i])

    loads = [
        pltpu.make_async_copy(source, target, load_sem.at[i])
        for i, (source, target) in enumerate(
            ((gather_hbm, gather), (weight_hbm, weight), (grad_hbm, grad), (moment_hbm, moment), (second_hbm, second))
        )
    ]
    loads[0].start()
    part_copy(0).start()
    loads[1].start()
    for i in range(1, parts):
        part_copy(i).start()
    for copy in loads[2:]:
        copy.start()
    loads[0].wait()
    tiles = []
    for t in range(n_mp // 2):
        top, bottom = halves(gather[2 * t].astype(F32), gather[2 * t + 1].astype(F32), low_lanes(32))
        tiles.append(jnp.concatenate([top, bottom], axis=0).astype(BF16))
    left = jnp.concatenate(tiles, axis=1)
    loads[1].wait()
    for i in range(parts):
        part_copy(i).wait()
        span = slice(i * DEPTH, (i + 1) * DEPTH)
        update = lax.dot_general(left, basis[span, :], (((1,), (1,)), ((), ())), preferred_element_type=F32)
        new_weight[:, span] = (weight[:, span].astype(F32) - step_size * update).astype(BF16)
        out_copy(i).start()
    for copy in loads[2:]:
        copy.wait()
    new_moment[...] = beta_first * moment[...] + (1.0 - beta_first) * grad[...]
    new_second[...] = beta_second * second[...] + (1.0 - beta_second) * grad[...] * grad[...]
    stores = [
        pltpu.make_async_copy(new_moment, moment_out, store_sem.at[0]),
        pltpu.make_async_copy(new_second, second_out, store_sem.at[1]),
    ]
    for copy in stores:
        copy.start()
    for i in range(parts):
        out_copy(i).wait()
    for copy in stores:
        copy.wait()


def shards(side, n_mp, activations, cotangent, subspace_basis, weight, moment, second):
    micro, tokens, width = activations.shape
    act = activations.reshape(micro * tokens, width)
    cot = cotangent.reshape(micro * tokens, cotangent.shape[2])
    units, rank = subspace_basis.shape
    dma = pltpu.SemaphoreType.DMA
    n = side - 1
    m = n_mp - 1
    block = (2, HALF, 128)
    plane = (side, HALF, 128)
    axis_recv = [
        pltpu.VMEM((2, 2) + plane, BF16),
        pltpu.VMEM((2, 2) + plane, BF16),
        pltpu.VMEM((2, 2) + plane, BF16),
        pltpu.VMEM((2,) + plane, BF16),
    ]
    scratch = [
        pltpu.VMEM(act.shape, BF16),
        pltpu.VMEM(cot.shape, BF16),
        pltpu.VMEM(subspace_basis.shape, BF16),
        pltpu.VMEM(moment.shape, F32),
        pltpu.VMEM(second.shape, F32),
        pltpu.VMEM(moment.shape, F32),
        pltpu.VMEM((micro * tokens, rank), F32),
        pltpu.VMEM((n_mp, tokens, 128), BF16),
        pltpu.VMEM((m, tokens, 128), BF16),
        pltpu.VMEM((OWN, 256), BF16),
        pltpu.VMEM((side, 2) + plane, BF16),
        pltpu.VMEM((side, 2) + plane, BF16),
        *axis_recv,
        *axis_recv,
        pltpu.VMEM((side,) + block, BF16),
        pltpu.VMEM((side,) + block, BF16),
        pltpu.VMEM((n,) + block, BF16),
        pltpu.VMEM((n,) + block, BF16),
        pltpu.VMEM((2, 32, 128), F32),
        pltpu.VMEM((32, 128), F32),
        pltpu.VMEM((n_mp, 32, 128), BF16),
        dma((3,)),
        dma((2, units // DEPTH)),
        dma((2,)),
        dma((m,)), dma((m,)),
        dma((4, 2)), dma((4, 2)), dma((4, 2)), dma((4, 2)),
        dma((n,)), dma((n,)), dma((n,)), dma((n,)),
        dma(()), dma(()),
        dma((m,)), dma((m,)),
    ]
    hbm = pl.BlockSpec(memory_space=pltpu.HBM)
    gathered, grad = pl.pallas_call(
        functools.partial(gradient_kernel, side, n_mp),
        out_shape=(
            jax.ShapeDtypeStruct((n_mp, 32, 128), BF16),
            jax.ShapeDtypeStruct(moment.shape, F32),
        ),
        in_specs=[hbm] * 5,
        out_specs=(hbm,) * 2,
        scratch_shapes=scratch,
        compiler_params=pltpu.CompilerParams(
            collective_id=0, has_side_effects=True, vmem_limit_bytes=60 * 1024 * 1024
        ),
    )(act, cot, subspace_basis, moment, second)
    return pl.pallas_call(
        functools.partial(weight_kernel, n_mp),
        out_shape=(
            jax.ShapeDtypeStruct(weight.shape, BF16),
            jax.ShapeDtypeStruct(moment.shape, F32),
            jax.ShapeDtypeStruct(second.shape, F32),
        ),
        in_specs=[hbm] * 6,
        out_specs=(hbm,) * 3,
        scratch_shapes=[
            pltpu.VMEM((n_mp, 32, 128), BF16),
            pltpu.VMEM(moment.shape, F32),
            pltpu.VMEM(subspace_basis.shape, BF16),
            pltpu.VMEM(weight.shape, BF16),
            pltpu.VMEM(moment.shape, F32),
            pltpu.VMEM(second.shape, F32),
            pltpu.VMEM(weight.shape, BF16),
            pltpu.VMEM(moment.shape, F32),
            pltpu.VMEM(second.shape, F32),
            dma((5,)),
            dma((2, units // DEPTH)),
            dma((2,)),
        ],
        compiler_params=pltpu.CompilerParams(vmem_limit_bytes=60 * 1024 * 1024),
    )(gathered, grad, subspace_basis, weight, moment, second)


def solution(mesh):
    side = math.isqrt(mesh.shape["dp"] // 2)
    n_mp = mesh.shape["mp"]
    in_specs = (
        P(None, "dp", None),
        P(None, "dp", "mp"),
        P("mp", None),
        P("dp", "mp"),
        P("dp", "mp"),
        P("dp", "mp"),
    )
    out_specs = (P("dp", "mp"), P("dp", "mp"), P("dp", "mp"))
    return jax.shard_map(
        functools.partial(shards, side, n_mp), mesh=mesh, in_specs=in_specs, out_specs=out_specs, check_vma=False
    )
```

```python
import functools
import math

import jax
import jax.numpy as jnp
from jax import lax
from jax.experimental import pallas as pl
from jax.experimental.pallas import tpu as pltpu
from jax.sharding import PartitionSpec as P

beta_first = 0.9
beta_second = 0.999
epsilon = 1e-08
step_size = 0.25

F32 = jnp.float32
BF16 = jnp.bfloat16
MESH_ID = pl.DeviceIdType.MESH
OWN = 64
HALF = 16
DEPTH = 512
VMEM = 60 * 1024 * 1024


def halves(top, bottom, low):
    first = jnp.where(low, top, pltpu.roll(bottom, 64, 1))
    second = jnp.where(low, pltpu.roll(top, 64, 1), bottom)
    return first, second


def far_first(n):
    return sorted(range(1, n), key=lambda k: (-min(k, n - k), k))


def low_lanes(rows):
    return lax.broadcasted_iota(jnp.int32, (rows, 128), 1) < 64


def step_kernel(
    side, n_mp, act_hbm, cot_hbm, basis_hbm, weight_hbm, moment_hbm, second_hbm,
    weight_out, moment_out, second_out,
    act, cot, basis, weight, moment, second, new_weight, new_moment, new_second,
    partial, mp_send, mp_recv, rows_t, y_send, z_send,
    y_recv1, y_recv2, y_recv3, y_recv4, z_recv1, z_recv2, z_recv3, z_recv4,
    zz_send, yy_send, zz_recv, yy_recv, gather,
    load_sem, part_sem, store_sem, mp_ss, mp_rs, y_ss, y_rs, z_ss, z_rs,
    zz_ss, zz_rs, yy_ss, yy_rs, g_ss, g_rs,
):
    dp = lax.axis_index("dp")
    mp = lax.axis_index("mp")
    y = lax.rem(dp, side)
    z = lax.rem(dp // side, side)
    x = dp // (side * side)

    def y_peer(k):
        return (dp - y + lax.rem(y + k, side), mp)

    def z_peer(k):
        return (dp + (lax.rem(z + k, side) - z) * side, mp)

    def mp_peer(k):
        return (dp, lax.rem(mp + k, n_mp))

    def xy_peer(k, flip):
        return (dp + flip * (1 - 2 * x) * side * side - y + lax.rem(y + k, side), mp)

    def xz_peer(k, flip):
        return (dp + flip * (1 - 2 * x) * side * side + (lax.rem(z + k, side) - z) * side, mp)

    def remote(src, dst, send_sem, recv_sem, device):
        return pltpu.make_async_remote_copy(
            src_ref=src, dst_ref=dst, send_sem=send_sem, recv_sem=recv_sem,
            device_id=device, device_id_type=MESH_ID,
        )

    tokens = act.shape[0]
    micro = tokens // 2
    parts = basis.shape[0] // DEPTH

    def part_copies(i):
        span = pl.ds(i * DEPTH, DEPTH)
        return (
            pltpu.make_async_copy(basis_hbm.at[span, :], basis.at[span, :], part_sem.at[0, i]),
            pltpu.make_async_copy(cot_hbm.at[:, span], cot.at[:, span], part_sem.at[1, i]),
        )

    for i in range(parts):
        for copy in part_copies(i):
            copy.start()
    loads = [
        pltpu.make_async_copy(act_hbm, act, load_sem.at[0]),
        pltpu.make_async_copy(moment_hbm, moment, load_sem.at[1]),
        pltpu.make_async_copy(second_hbm, second, load_sem.at[2]),
        pltpu.make_async_copy(weight_hbm, weight, load_sem.at[3]),
    ]
    for copy in loads:
        copy.start()

    barrier = pltpu.get_barrier_semaphore()
    for k in range(1, n_mp):
        pl.semaphore_signal(barrier, inc=1, device_id=mp_peer(k), device_id_type=MESH_ID)
    for flip in range(2):
        for k in range(1, side):
            pl.semaphore_signal(barrier, inc=1, device_id=xy_peer(k, flip), device_id_type=MESH_ID)
            pl.semaphore_signal(barrier, inc=1, device_id=xz_peer(k, flip), device_id_type=MESH_ID)
    pl.semaphore_signal(barrier, inc=1, device_id=xy_peer(0, 1), device_id_type=MESH_ID)

    for i in range(parts):
        for copy in part_copies(i):
            copy.wait()
        span = slice(i * DEPTH, (i + 1) * DEPTH)
        term = jnp.dot(cot[:, span], basis[span, :], preferred_element_type=F32)
        if i == 0:
            partial[...] = term
        else:
            partial[...] += term

    for t in range(n_mp // 2):
        cols = slice(t * 128, (t + 1) * 128)
        first, other = halves(partial[:micro, cols], partial[micro:, cols], low_lanes(micro))
        mp_send[2 * t] = first.astype(BF16)
        mp_send[2 * t + 1] = other.astype(BF16)

    pl.semaphore_wait(barrier, n_mp - 1 + 4 * (side - 1) + 1)

    def mp_copy(k):
        return remote(
            mp_send.at[lax.rem(mp + k, n_mp)], mp_recv.at[k - 1], mp_ss.at[k - 1], mp_rs.at[k - 1], mp_peer(k)
        )

    for k in far_first(n_mp):
        mp_copy(k).start()
    total = mp_send[mp].astype(F32)
    for k in reversed(far_first(n_mp)):
        mp_copy(k).wait_recv()
        total = total + mp_recv[k - 1].astype(F32)
    projected = total.astype(BF16).astype(F32)
    stacked = jnp.concatenate(
        [projected, pltpu.roll(projected, 64, 1), jnp.zeros((256 - tokens, 128), F32)], axis=0
    )
    rows_t[...] = stacked.T[:OWN, :].astype(BF16)

    loads[0].wait()
    y_lhs = rows_t[:32, :tokens]
    z_lhs = rows_t[32:, :tokens]
    width = side * OWN

    def z_blocks(offset):
        to_z = lax.rem(z + offset, side)
        for to_x in range(2):
            start = pl.multiple_of((to_x * side + to_z) * width, 128)
            grad = jnp.dot(z_lhs, act[:, pl.ds(start, width)], preferred_element_type=F32)
            for pair in range(side // 2):
                tile = grad[:, pair * 128 : (pair + 1) * 128]
                for lo, block in enumerate(halves(tile[:HALF], tile[HALF:], low_lanes(HALF))):
                    z_send[to_z, to_x, 2 * pair + lo] = block.astype(BF16)

    def y_blocks(offset):
        pair = lax.rem(y // 2 + offset, side // 2)
        for to_x in range(2):
            for q in range(side // 2):
                tiles = []
                for to_z in (2 * q, 2 * q + 1):
                    start = pl.multiple_of((to_x * side + to_z) * width + pair * 128, 128)
                    tiles.append(act[:, pl.ds(start, 128)])
                grad = jnp.dot(y_lhs, jnp.concatenate(tiles, axis=1), preferred_element_type=F32)
                for r in range(2):
                    tile = grad[:, r * 128 : (r + 1) * 128]
                    for lo, block in enumerate(halves(tile[:HALF], tile[HALF:], low_lanes(HALF))):
                        y_send[2 * pair + lo, to_x, 2 * q + r] = block.astype(BF16)

    def axis(pos, peer, send, recv1, recv2, recv3, recv4, ss, rs):
        def block(offset):
            return send.at[lax.rem(pos + offset, side)]

        up, down = (1, 2, 3), (side - 1, side - 2, side - 3)
        near, merged, far, across = [], [], [], []
        for way, (one, two, three) in enumerate((up, down)):
            near.append(remote(block(one), recv1.at[way], ss.at[0, way], rs.at[0, way], peer(one)))
            merged.append(remote(block(two), recv2.at[way], ss.at[1, way], rs.at[1, way], peer(two)))
            far.append(remote(block(three), recv3.at[way], ss.at[2, way], rs.at[2, way], peer(one)))
            across.append(remote(block(4).at[way], recv4.at[way], ss.at[3, way], rs.at[3, way], peer(two)))

        def merge():
            for way, two in enumerate((2, side - 2)):
                slot = lax.rem(pos + two, side)
                far[way].wait_recv()
                across[way].wait_recv()
                for to_x in range(2):
                    acc = send[slot, to_x].astype(F32) + recv3[way, to_x].astype(F32)
                    if to_x == way:
                        acc = acc + recv4[way].astype(F32)
                    send[slot, to_x] = acc.astype(BF16)
                merged[way].start()

        def total(out):
            for way in range(2):
                near[way].wait_recv()
                merged[way].wait_recv()
            for to_x in range(2):
                acc = send[pos, to_x].astype(F32)
                for recv in (recv1, recv2):
                    for way in range(2):
                        acc = acc + recv[way, to_x].astype(F32)
                acc = acc.astype(BF16)
                for q in range(side):
                    out[q, to_x] = acc[q]

        return near, merged, far, across, merge, total

    z_near, z_merged, z_far, z_across, z_merge, z_total = axis(
        z, z_peer, z_send, z_recv1, z_recv2, z_recv3, z_recv4, z_ss, z_rs
    )
    y_near, y_merged, y_far, y_across, y_merge, y_total = axis(
        y, y_peer, y_send, y_recv1, y_recv2, y_recv3, y_recv4, y_ss, y_rs
    )

    def begin(copies):
        for copy in copies:
            copy.start()

    z_blocks(4)
    begin(z_across)
    z_blocks(3)
    z_blocks(side - 3)
    begin(z_far)
    y_blocks(2)
    begin(y_across)
    y_blocks(1)
    y_blocks(3)
    begin(y_far)
    z_blocks(1)
    z_blocks(side - 1)
    begin(z_near)
    y_blocks(0)
    begin(y_near)
    z_blocks(2)
    z_blocks(side - 2)
    z_merge()
    y_merge()
    z_blocks(0)

    targets = [(k, flip) for k in far_first(side) for flip in (1, 0)] + [(0, 1)]

    def second_copies(pos, peer, send, recv, ss, rs):
        return [
            remote(
                send.at[lax.rem(pos + k, side), x + flip * (1 - 2 * x)],
                recv.at[i], ss.at[i], rs.at[i], peer(k, flip),
            )
            for i, (k, flip) in enumerate(targets)
        ]

    yy_copies = second_copies(y, xy_peer, yy_send, yy_recv, yy_ss, yy_rs)
    zz_copies = second_copies(z, xz_peer, zz_send, zz_recv, zz_ss, zz_rs)
    z_total(yy_send)
    begin(yy_copies)
    y_total(zz_send)
    begin(zz_copies)

    def add_second(copies, send, recv, own):
        acc = send[own, x].astype(F32)
        for i in reversed(range(len(copies))):
            copies[i].wait_recv()
            acc = acc + recv[i].astype(F32)
        return acc

    z_half = add_second(yy_copies, yy_send, yy_recv, y)
    y_half = add_second(zz_copies, zz_send, zz_recv, z)
    grad_t = jnp.concatenate([y_half, pltpu.roll(y_half, 64, 1), z_half, pltpu.roll(z_half, 64, 1)], axis=0)
    grad = grad_t.T[:OWN, :]

    loads[1].wait()
    loads[2].wait()
    moment_new = beta_first * moment[...] + (1.0 - beta_first) * grad
    second_new = beta_second * second[...] + (1.0 - beta_second) * grad * grad
    new_moment[...] = moment_new
    new_second[...] = second_new
    direction = moment_new / (jnp.sqrt(second_new) + epsilon)
    gather[mp] = jnp.concatenate([direction[:32], direction[32:]], axis=1).astype(BF16)

    def g_copy(k):
        return remote(gather.at[mp], gather.at[mp], g_ss.at[k - 1], g_rs.at[k - 1], mp_peer(k))

    def g_arrival(k):
        slot = lax.rem(mp + n_mp - k, n_mp)
        return remote(gather.at[slot], gather.at[slot], g_ss.at[k - 1], g_rs.at[k - 1], mp_peer(k))

    for k in far_first(n_mp):
        g_copy(k).start()
    stores = [
        pltpu.make_async_copy(new_moment, moment_out, store_sem.at[0]),
        pltpu.make_async_copy(new_second, second_out, store_sem.at[1]),
    ]
    begin(stores)
    for k in range(1, n_mp):
        mp_copy(k).wait_send()
    for copies in (z_near, z_merged, z_far, z_across, y_near, y_merged, y_far, y_across, yy_copies, zz_copies):
        for copy in copies:
            copy.wait_send()
    loads[3].wait()
    for k in reversed(far_first(n_mp)):
        g_arrival(k).wait_recv()
    tiles = []
    for t in range(n_mp // 2):
        top, bottom = halves(gather[2 * t].astype(F32), gather[2 * t + 1].astype(F32), low_lanes(32))
        tiles.append(jnp.concatenate([top, bottom], axis=0).astype(BF16))
    left = jnp.concatenate(tiles, axis=1)
    for i in range(parts):
        span = slice(i * DEPTH, (i + 1) * DEPTH)
        update = lax.dot_general(left, basis[span, :], (((1,), (1,)), ((), ())), preferred_element_type=F32)
        new_weight[:, span] = (weight[:, span].astype(F32) - step_size * update).astype(BF16)
        stores.append(pltpu.make_async_copy(new_weight.at[:, span], weight_out.at[:, span], store_sem.at[2 + i]))
        stores[-1].start()
    for k in range(1, n_mp):
        g_copy(k).wait_send()
    for copy in stores:
        copy.wait()


def copy_kernel(*refs):
    count = (len(refs) - 1) // 2
    copies = [pltpu.make_async_copy(refs[i], refs[count + i], refs[-1].at[i]) for i in range(count)]
    for copy in copies:
        copy.start()
    for copy in copies:
        copy.wait()


def shards(side, n_mp, activations, cotangent, subspace_basis, weight, moment, second):
    micro, tokens, width = activations.shape
    act = activations.reshape(micro * tokens, width)
    cot = cotangent.reshape(micro * tokens, cotangent.shape[2])
    units, rank = subspace_basis.shape
    dma = pltpu.SemaphoreType.DMA
    m = n_mp - 1
    n2 = 2 * side - 1
    plane = (side, HALF, 128)
    axis_recv = [
        pltpu.VMEM((2, 2) + plane, BF16),
        pltpu.VMEM((2, 2) + plane, BF16),
        pltpu.VMEM((2, 2) + plane, BF16),
        pltpu.VMEM((2,) + plane, BF16),
    ]
    scratch = [
        pltpu.VMEM(act.shape, BF16),
        pltpu.VMEM(cot.shape, BF16),
        pltpu.VMEM(subspace_basis.shape, BF16),
        pltpu.VMEM(weight.shape, BF16),
        pltpu.VMEM(moment.shape, F32),
        pltpu.VMEM(second.shape, F32),
        pltpu.VMEM(weight.shape, BF16),
        pltpu.VMEM(moment.shape, F32),
        pltpu.VMEM(second.shape, F32),
        pltpu.VMEM((micro * tokens, rank), F32),
        pltpu.VMEM((n_mp, tokens, 128), BF16),
        pltpu.VMEM((m, tokens, 128), BF16),
        pltpu.VMEM((OWN, 256), BF16),
        pltpu.VMEM((side, 2) + plane, BF16),
        pltpu.VMEM((side, 2) + plane, BF16),
        *axis_recv,
        *axis_recv,
        pltpu.VMEM((side, 2, HALF, 128), BF16),
        pltpu.VMEM((side, 2, HALF, 128), BF16),
        pltpu.VMEM((n2, HALF, 128), BF16),
        pltpu.VMEM((n2, HALF, 128), BF16),
        pltpu.VMEM((n_mp, 32, 128), BF16),
        dma((4,)),
        dma((2, units // DEPTH)),
        dma((2 + units // DEPTH,)),
        dma((m,)), dma((m,)),
        dma((4, 2)), dma((4, 2)), dma((4, 2)), dma((4, 2)),
        dma((n2,)), dma((n2,)), dma((n2,)), dma((n2,)),
        dma((m,)), dma((m,)),
    ]
    hbm = pl.BlockSpec(memory_space=pltpu.HBM)
    shapes = tuple(jax.ShapeDtypeStruct(a.shape, a.dtype) for a in (weight, moment, second))
    results = pl.pallas_call(
        functools.partial(step_kernel, side, n_mp),
        out_shape=shapes,
        in_specs=[hbm] * 6,
        out_specs=(hbm,) * 3,
        scratch_shapes=scratch,
        compiler_params=pltpu.CompilerParams(
            collective_id=0, has_side_effects=True, vmem_limit_bytes=VMEM
        ),
    )(act, cot, subspace_basis, weight, moment, second)
    return pl.pallas_call(
        copy_kernel,
        out_shape=shapes,
        in_specs=[hbm] * 3,
        out_specs=(hbm,) * 3,
        scratch_shapes=[dma((3,))],
        compiler_params=pltpu.CompilerParams(vmem_limit_bytes=VMEM),
    )(*results)


def solution(mesh):
    side = math.isqrt(mesh.shape["dp"] // 2)
    n_mp = mesh.shape["mp"]
    in_specs = (
        P(None, "dp", None),
        P(None, "dp", "mp"),
        P("mp", None),
        P("dp", "mp"),
        P("dp", "mp"),
        P("dp", "mp"),
    )
    out_specs = (P("dp", "mp"), P("dp", "mp"), P("dp", "mp"))
    return jax.shard_map(
        functools.partial(shards, side, n_mp), mesh=mesh, in_specs=in_specs, out_specs=out_specs, check_vma=False
    )
```

```python
import functools
import math

import jax
import jax.numpy as jnp
from jax import lax
from jax.experimental import pallas as pl
from jax.experimental.pallas import tpu as pltpu
from jax.sharding import PartitionSpec as P

beta_first = 0.9
beta_second = 0.999
epsilon = 1e-08
step_size = 0.25

F32 = jnp.float32
BF16 = jnp.bfloat16
MESH_ID = pl.DeviceIdType.MESH
OWN = 64
HALF = 16
DEPTH = 512
VMEM = 60 * 1024 * 1024


def halves(top, bottom, low):
    first = jnp.where(low, top, pltpu.roll(bottom, 64, 1))
    second = jnp.where(low, pltpu.roll(top, 64, 1), bottom)
    return first, second


def far_first(n):
    return sorted(range(1, n), key=lambda k: (-min(k, n - k), k))


def low_lanes(rows):
    return lax.broadcasted_iota(jnp.int32, (rows, 128), 1) < 64


def step_kernel(
    side, n_mp, act_hbm, cot_hbm, basis_hbm, weight_hbm, moment_hbm, second_hbm,
    weight_out, moment_out, second_out,
    act, cot, basis, weight, moment, second, half_weight, new_weight, new_moment, new_second,
    partial, mp_send, mp_recv, rows_t, y_send, z_send,
    y_recv1, y_recv2, y_recv3, y_recv4, z_recv1, z_recv2, z_recv3, z_recv4,
    zz_send, yy_send, zz_recv, yy_recv, gather,
    load_sem, part_sem, store_sem, mp_ss, mp_rs, y_ss, y_rs, z_ss, z_rs,
    zz_ss, zz_rs, yy_ss, yy_rs, g_ss, g_rs,
):
    dp = lax.axis_index("dp")
    mp = lax.axis_index("mp")
    y = lax.rem(dp, side)
    z = lax.rem(dp // side, side)
    x = dp // (side * side)

    def y_peer(k):
        return (dp - y + lax.rem(y + k, side), mp)

    def z_peer(k):
        return (dp + (lax.rem(z + k, side) - z) * side, mp)

    def mp_peer(k):
        return (dp, lax.rem(mp + k, n_mp))

    def xy_peer(k, flip):
        return (dp + flip * (1 - 2 * x) * side * side - y + lax.rem(y + k, side), mp)

    def xz_peer(k, flip):
        return (dp + flip * (1 - 2 * x) * side * side + (lax.rem(z + k, side) - z) * side, mp)

    def remote(src, dst, send_sem, recv_sem, device):
        return pltpu.make_async_remote_copy(
            src_ref=src, dst_ref=dst, send_sem=send_sem, recv_sem=recv_sem,
            device_id=device, device_id_type=MESH_ID,
        )

    tokens = act.shape[0]
    micro = tokens // 2
    parts = basis.shape[0] // DEPTH

    def part_copies(i):
        span = pl.ds(i * DEPTH, DEPTH)
        return (
            pltpu.make_async_copy(basis_hbm.at[span, :], basis.at[span, :], part_sem.at[0, i]),
            pltpu.make_async_copy(cot_hbm.at[:, span], cot.at[:, span], part_sem.at[1, i]),
        )

    for i in range(parts):
        for copy in part_copies(i):
            copy.start()
    loads = [
        pltpu.make_async_copy(act_hbm, act, load_sem.at[0]),
        pltpu.make_async_copy(moment_hbm, moment, load_sem.at[1]),
        pltpu.make_async_copy(second_hbm, second, load_sem.at[2]),
        pltpu.make_async_copy(weight_hbm, weight, load_sem.at[3]),
    ]
    for copy in loads:
        copy.start()

    barrier = pltpu.get_barrier_semaphore()
    for k in range(1, n_mp):
        pl.semaphore_signal(barrier, inc=1, device_id=mp_peer(k), device_id_type=MESH_ID)
    for flip in range(2):
        for k in range(1, side):
            pl.semaphore_signal(barrier, inc=1, device_id=xy_peer(k, flip), device_id_type=MESH_ID)
            pl.semaphore_signal(barrier, inc=1, device_id=xz_peer(k, flip), device_id_type=MESH_ID)
    pl.semaphore_signal(barrier, inc=1, device_id=xy_peer(0, 1), device_id_type=MESH_ID)

    for i in range(parts):
        for copy in part_copies(i):
            copy.wait()
        span = slice(i * DEPTH, (i + 1) * DEPTH)
        term = jnp.dot(cot[:, span], basis[span, :], preferred_element_type=F32)
        if i == 0:
            partial[...] = term
        else:
            partial[...] += term

    for t in range(n_mp // 2):
        cols = slice(t * 128, (t + 1) * 128)
        first, other = halves(partial[:micro, cols], partial[micro:, cols], low_lanes(micro))
        mp_send[2 * t] = first.astype(BF16)
        mp_send[2 * t + 1] = other.astype(BF16)

    pl.semaphore_wait(barrier, n_mp - 1 + 4 * (side - 1) + 1)

    def mp_copy(k):
        return remote(
            mp_send.at[lax.rem(mp + k, n_mp)], mp_recv.at[k - 1], mp_ss.at[k - 1], mp_rs.at[k - 1], mp_peer(k)
        )

    for k in far_first(n_mp):
        mp_copy(k).start()
    total = mp_send[mp].astype(F32)
    for k in reversed(far_first(n_mp)):
        mp_copy(k).wait_recv()
        total = total + mp_recv[k - 1].astype(F32)
    projected = total.astype(BF16).astype(F32)
    stacked = jnp.concatenate(
        [projected, pltpu.roll(projected, 64, 1), jnp.zeros((256 - tokens, 128), F32)], axis=0
    )
    rows_t[...] = stacked.T[:OWN, :].astype(BF16)

    loads[0].wait()
    y_lhs = rows_t[:32, :tokens]
    z_lhs = rows_t[32:, :tokens]
    width = side * OWN

    def z_blocks(offset):
        to_z = lax.rem(z + offset, side)
        for to_x in range(2):
            start = pl.multiple_of((to_x * side + to_z) * width, 128)
            grad = jnp.dot(z_lhs, act[:, pl.ds(start, width)], preferred_element_type=F32)
            for pair in range(side // 2):
                tile = grad[:, pair * 128 : (pair + 1) * 128]
                for lo, block in enumerate(halves(tile[:HALF], tile[HALF:], low_lanes(HALF))):
                    z_send[to_z, to_x, 2 * pair + lo] = block.astype(BF16)

    def y_blocks(offset):
        pair = lax.rem(y // 2 + offset, side // 2)
        for to_x in range(2):
            for q in range(side // 2):
                tiles = []
                for to_z in (2 * q, 2 * q + 1):
                    start = pl.multiple_of((to_x * side + to_z) * width + pair * 128, 128)
                    tiles.append(act[:, pl.ds(start, 128)])
                grad = jnp.dot(y_lhs, jnp.concatenate(tiles, axis=1), preferred_element_type=F32)
                for r in range(2):
                    tile = grad[:, r * 128 : (r + 1) * 128]
                    for lo, block in enumerate(halves(tile[:HALF], tile[HALF:], low_lanes(HALF))):
                        y_send[2 * pair + lo, to_x, 2 * q + r] = block.astype(BF16)

    def axis(pos, peer, send, recv1, recv2, recv3, recv4, ss, rs):
        def block(offset):
            return send.at[lax.rem(pos + offset, side)]

        up, down = (1, 2, 3), (side - 1, side - 2, side - 3)
        near, merged, far, across = [], [], [], []
        for way, (one, two, three) in enumerate((up, down)):
            near.append(remote(block(one), recv1.at[way], ss.at[0, way], rs.at[0, way], peer(one)))
            merged.append(remote(block(two), recv2.at[way], ss.at[1, way], rs.at[1, way], peer(two)))
            far.append(remote(block(three), recv3.at[way], ss.at[2, way], rs.at[2, way], peer(one)))
            across.append(remote(block(4).at[way], recv4.at[way], ss.at[3, way], rs.at[3, way], peer(two)))

        def merge():
            for way, two in enumerate((2, side - 2)):
                slot = lax.rem(pos + two, side)
                far[way].wait_recv()
                across[way].wait_recv()
                for to_x in range(2):
                    acc = send[slot, to_x].astype(F32) + recv3[way, to_x].astype(F32)
                    if to_x == way:
                        acc = acc + recv4[way].astype(F32)
                    send[slot, to_x] = acc.astype(BF16)
                merged[way].start()

        def total(out):
            for way in range(2):
                near[way].wait_recv()
                merged[way].wait_recv()
            for to_x in range(2):
                acc = send[pos, to_x].astype(F32)
                for recv in (recv1, recv2):
                    for way in range(2):
                        acc = acc + recv[way, to_x].astype(F32)
                acc = acc.astype(BF16)
                for q in range(side):
                    out[q, to_x] = acc[q]

        return near, merged, far, across, merge, total

    z_near, z_merged, z_far, z_across, z_merge, z_total = axis(
        z, z_peer, z_send, z_recv1, z_recv2, z_recv3, z_recv4, z_ss, z_rs
    )
    y_near, y_merged, y_far, y_across, y_merge, y_total = axis(
        y, y_peer, y_send, y_recv1, y_recv2, y_recv3, y_recv4, y_ss, y_rs
    )

    def begin(copies):
        for copy in copies:
            copy.start()

    z_blocks(4)
    begin(z_across)
    z_blocks(3)
    z_blocks(side - 3)
    begin(z_far)
    y_blocks(2)
    begin(y_across)
    y_blocks(1)
    y_blocks(3)
    begin(y_far)
    z_blocks(1)
    z_blocks(side - 1)
    begin(z_near)
    y_blocks(0)
    begin(y_near)
    z_blocks(2)
    z_blocks(side - 2)
    z_merge()
    y_merge()
    z_blocks(0)

    targets = [(k, flip) for k in far_first(side) for flip in (1, 0)] + [(0, 1)]

    def second_copies(pos, peer, send, recv, ss, rs):
        return [
            remote(
                send.at[lax.rem(pos + k, side), x + flip * (1 - 2 * x)],
                recv.at[i], ss.at[i], rs.at[i], peer(k, flip),
            )
            for i, (k, flip) in enumerate(targets)
        ]

    yy_copies = second_copies(y, xy_peer, yy_send, yy_recv, yy_ss, yy_rs)
    zz_copies = second_copies(z, xz_peer, zz_send, zz_recv, zz_ss, zz_rs)
    z_total(yy_send)
    begin(yy_copies)
    y_total(zz_send)
    begin(zz_copies)

    def add_second(copies, send, recv, own):
        acc = send[own, x].astype(F32)
        for i in reversed(range(len(copies))):
            copies[i].wait_recv()
            acc = acc + recv[i].astype(F32)
        return acc

    z_half = add_second(yy_copies, yy_send, yy_recv, y)
    y_half = add_second(zz_copies, zz_send, zz_recv, z)
    grad_t = jnp.concatenate([y_half, pltpu.roll(y_half, 64, 1), z_half, pltpu.roll(z_half, 64, 1)], axis=0)
    grad = grad_t.T[:OWN, :]

    loads[1].wait()
    loads[2].wait()
    moment_new = beta_first * moment[...] + (1.0 - beta_first) * grad
    second_new = beta_second * second[...] + (1.0 - beta_second) * grad * grad
    new_moment[...] = moment_new
    new_second[...] = second_new
    direction = moment_new / (jnp.sqrt(second_new) + epsilon)
    gather[mp] = jnp.concatenate([direction[:32], direction[32:]], axis=1).astype(BF16)

    def g_copy(k):
        return remote(gather.at[mp], gather.at[mp], g_ss.at[k - 1], g_rs.at[k - 1], mp_peer(k))

    for k in far_first(n_mp):
        g_copy(k).start()
    stores = [
        pltpu.make_async_copy(new_moment, moment_out, store_sem.at[0]),
        pltpu.make_async_copy(new_second, second_out, store_sem.at[1]),
    ]
    begin(stores)
    for k in range(1, n_mp):
        mp_copy(k).wait_send()
    for copies in (z_near, z_merged, z_far, z_across, y_near, y_merged, y_far, y_across, yy_copies, zz_copies):
        for copy in copies:
            copy.wait_send()
    loads[3].wait()

    def pair_of(steps):
        return lax.rem(mp // 2 + steps, n_mp // 2)

    def pair_tile(pair):
        top, bottom = halves(gather[2 * pair].astype(F32), gather[2 * pair + 1].astype(F32), low_lanes(32))
        return jnp.concatenate([top, bottom], axis=0).astype(BF16)

    def arrivals(pairs):
        for steps in pairs:
            for core in range(2):
                slot = 2 * pair_of(steps) + core
                k = lax.rem(mp + n_mp - slot, n_mp)

                @pl.when(k > 0)
                def _():
                    remote(gather.at[slot], gather.at[slot], g_ss.at[0], g_rs.at[k - 1], mp_peer(1)).wait_recv()

    pairs = n_mp // 2
    near_pairs, far_pairs = (0, 1), (pairs - 1, pairs - 2)
    for stage, group in enumerate((near_pairs, far_pairs)):
        arrivals(group)
        left = jnp.concatenate([pair_tile(pair_of(steps)) for steps in group], axis=1)
        columns = [pl.ds(pl.multiple_of(pair_of(steps) * 128, 128), 128) for steps in group]
        for i in range(parts):
            span = slice(i * DEPTH, (i + 1) * DEPTH)
            right = jnp.concatenate([basis[span, cols] for cols in columns], axis=1)
            update = lax.dot_general(left, right, (((1,), (1,)), ((), ())), preferred_element_type=F32)
            if stage == 0:
                half_weight[:, span] = weight[:, span].astype(F32) - step_size * update
            else:
                new_weight[:, span] = (half_weight[:, span] - step_size * update).astype(BF16)
                stores.append(pltpu.make_async_copy(new_weight.at[:, span], weight_out.at[:, span], store_sem.at[2 + i]))
                stores[-1].start()
    for k in range(1, n_mp):
        g_copy(k).wait_send()
    for copy in stores:
        copy.wait()


def copy_kernel(weight_in, moment_in, second_in, weight_out, moment_out, second_out, weight, moment, second, load_sem, store_sem):
    rows = [pl.ds(start, HALF) for start in range(0, OWN, HALF)]
    pieces = [(weight_in.at[r], weight.at[r], weight_out.at[r]) for r in rows]
    pieces += [(moment_in, moment, moment_out), (second_in, second, second_out)]
    loads = [pltpu.make_async_copy(a, b, load_sem.at[i]) for i, (a, b, _) in enumerate(pieces)]
    stores = [pltpu.make_async_copy(b, c, store_sem.at[i]) for i, (_, b, c) in enumerate(pieces)]
    for copy in loads:
        copy.start()
    for load, store in zip(loads, stores):
        load.wait()
        store.start()
    for copy in stores:
        copy.wait()


def shards(side, n_mp, activations, cotangent, subspace_basis, weight, moment, second):
    micro, tokens, width = activations.shape
    act = activations.reshape(micro * tokens, width)
    cot = cotangent.reshape(micro * tokens, cotangent.shape[2])
    units, rank = subspace_basis.shape
    dma = pltpu.SemaphoreType.DMA
    m = n_mp - 1
    n2 = 2 * side - 1
    plane = (side, HALF, 128)
    axis_recv = [
        pltpu.VMEM((2, 2) + plane, BF16),
        pltpu.VMEM((2, 2) + plane, BF16),
        pltpu.VMEM((2, 2) + plane, BF16),
        pltpu.VMEM((2,) + plane, BF16),
    ]
    scratch = [
        pltpu.VMEM(act.shape, BF16),
        pltpu.VMEM(cot.shape, BF16),
        pltpu.VMEM(subspace_basis.shape, BF16),
        pltpu.VMEM(weight.shape, BF16),
        pltpu.VMEM(moment.shape, F32),
        pltpu.VMEM(second.shape, F32),
        pltpu.VMEM(weight.shape, F32),
        pltpu.VMEM(weight.shape, BF16),
        pltpu.VMEM(moment.shape, F32),
        pltpu.VMEM(second.shape, F32),
        pltpu.VMEM((micro * tokens, rank), F32),
        pltpu.VMEM((n_mp, tokens, 128), BF16),
        pltpu.VMEM((m, tokens, 128), BF16),
        pltpu.VMEM((OWN, 256), BF16),
        pltpu.VMEM((side, 2) + plane, BF16),
        pltpu.VMEM((side, 2) + plane, BF16),
        *axis_recv,
        *axis_recv,
        pltpu.VMEM((side, 2, HALF, 128), BF16),
        pltpu.VMEM((side, 2, HALF, 128), BF16),
        pltpu.VMEM((n2, HALF, 128), BF16),
        pltpu.VMEM((n2, HALF, 128), BF16),
        pltpu.VMEM((n_mp, 32, 128), BF16),
        dma((4,)),
        dma((2, units // DEPTH)),
        dma((2 + units // DEPTH,)),
        dma((m,)), dma((m,)),
        dma((4, 2)), dma((4, 2)), dma((4, 2)), dma((4, 2)),
        dma((n2,)), dma((n2,)), dma((n2,)), dma((n2,)),
        dma((m,)), dma((m,)),
    ]
    hbm = pl.BlockSpec(memory_space=pltpu.HBM)
    shapes = tuple(jax.ShapeDtypeStruct(a.shape, a.dtype) for a in (weight, moment, second))
    results = pl.pallas_call(
        functools.partial(step_kernel, side, n_mp),
        out_shape=shapes,
        in_specs=[hbm] * 6,
        out_specs=(hbm,) * 3,
        scratch_shapes=scratch,
        compiler_params=pltpu.CompilerParams(
            collective_id=0, has_side_effects=True, vmem_limit_bytes=VMEM
        ),
    )(act, cot, subspace_basis, weight, moment, second)
    return pl.pallas_call(
        copy_kernel,
        out_shape=shapes,
        in_specs=[hbm] * 3,
        out_specs=(hbm,) * 3,
        scratch_shapes=[pltpu.VMEM(a.shape, a.dtype) for a in shapes]
        + [dma((2 + OWN // HALF,)), dma((2 + OWN // HALF,))],
        compiler_params=pltpu.CompilerParams(vmem_limit_bytes=VMEM),
    )(*results)


def solution(mesh):
    side = math.isqrt(mesh.shape["dp"] // 2)
    n_mp = mesh.shape["mp"]
    in_specs = (
        P(None, "dp", None),
        P(None, "dp", "mp"),
        P("mp", None),
        P("dp", "mp"),
        P("dp", "mp"),
        P("dp", "mp"),
    )
    out_specs = (P("dp", "mp"), P("dp", "mp"), P("dp", "mp"))
    return jax.shard_map(
        functools.partial(shards, side, n_mp), mesh=mesh, in_specs=in_specs, out_specs=out_specs, check_vma=False
    )
```

```python
import functools
import math

import jax
import jax.numpy as jnp
from jax import lax
from jax.experimental import pallas as pl
from jax.experimental.pallas import tpu as pltpu
from jax.sharding import PartitionSpec as P

beta_first = 0.9
beta_second = 0.999
epsilon = 1e-08
step_size = 0.25

F32 = jnp.float32
BF16 = jnp.bfloat16
MESH_ID = pl.DeviceIdType.MESH
OWN = 64
HALF = 16
DEPTH = 512
VMEM = 60 * 1024 * 1024


def halves(top, bottom, low):
    first = jnp.where(low, top, pltpu.roll(bottom, 64, 1))
    second = jnp.where(low, pltpu.roll(top, 64, 1), bottom)
    return first, second


def far_first(n):
    return sorted(range(1, n), key=lambda k: (-min(k, n - k), k))


def low_lanes(rows):
    return lax.broadcasted_iota(jnp.int32, (rows, 128), 1) < 64


def step_kernel(
    side, n_mp, act_hbm, cot_hbm, basis_hbm, weight_hbm, moment_hbm, second_hbm,
    weight_out, moment_out, second_out,
    act, cot, basis, weight, moment, second, half_weight, new_weight, new_moment, new_second,
    partial, mp_send, mp_recv, rows_t, y_send, z_send,
    y_recv1, y_recv2, y_recv3, y_recv4, z_recv1, z_recv2, z_recv3, z_recv4,
    zz_send, yy_send, zz_recv, yy_recv, gather,
    load_sem, part_sem, store_sem, mp_ss, mp_rs, y_ss, y_rs, z_ss, z_rs,
    zz_ss, zz_rs, yy_ss, yy_rs, g_ss, g_rs,
):
    dp = lax.axis_index("dp")
    mp = lax.axis_index("mp")
    y = lax.rem(dp, side)
    z = lax.rem(dp // side, side)
    x = dp // (side * side)

    def y_peer(k):
        return (dp - y + lax.rem(y + k, side), mp)

    def z_peer(k):
        return (dp + (lax.rem(z + k, side) - z) * side, mp)

    def mp_peer(k):
        return (dp, lax.rem(mp + k, n_mp))

    def xy_peer(k, flip):
        return (dp + flip * (1 - 2 * x) * side * side - y + lax.rem(y + k, side), mp)

    def xz_peer(k, flip):
        return (dp + flip * (1 - 2 * x) * side * side + (lax.rem(z + k, side) - z) * side, mp)

    def remote(src, dst, send_sem, recv_sem, device):
        return pltpu.make_async_remote_copy(
            src_ref=src, dst_ref=dst, send_sem=send_sem, recv_sem=recv_sem,
            device_id=device, device_id_type=MESH_ID,
        )

    tokens = act.shape[0]
    micro = tokens // 2
    parts = basis.shape[0] // DEPTH

    def part_copies(i):
        span = pl.ds(i * DEPTH, DEPTH)
        return (
            pltpu.make_async_copy(basis_hbm.at[span, :], basis.at[span, :], part_sem.at[0, i]),
            pltpu.make_async_copy(cot_hbm.at[:, span], cot.at[:, span], part_sem.at[1, i]),
        )

    early = parts // 2
    for i in range(early):
        for copy in part_copies(i):
            copy.start()

    barrier = pltpu.get_barrier_semaphore()
    peers = [xz_peer(k, flip) for flip in range(2) for k in range(1, side)]
    peers += [xy_peer(k, flip) for flip in (1, 0) for k in range(1 - flip, side)]
    peers += [mp_peer(k) for k in range(1, n_mp)]
    for peer in peers:
        pl.semaphore_signal(barrier, inc=1, device_id=peer, device_id_type=MESH_ID)

    for i in range(early, parts):
        for copy in part_copies(i):
            copy.start()
    loads = [
        pltpu.make_async_copy(act_hbm, act, load_sem.at[0]),
        pltpu.make_async_copy(moment_hbm, moment, load_sem.at[1]),
        pltpu.make_async_copy(second_hbm, second, load_sem.at[2]),
        pltpu.make_async_copy(weight_hbm, weight, load_sem.at[3]),
    ]
    for copy in loads:
        copy.start()

    for i in range(parts):
        for copy in part_copies(i):
            copy.wait()
        span = slice(i * DEPTH, (i + 1) * DEPTH)
        term = jnp.dot(cot[:, span], basis[span, :], preferred_element_type=F32)
        if i == 0:
            partial[...] = term
        else:
            partial[...] += term

    for t in range(n_mp // 2):
        cols = slice(t * 128, (t + 1) * 128)
        first, other = halves(partial[:micro, cols], partial[micro:, cols], low_lanes(micro))
        mp_send[2 * t] = first.astype(BF16)
        mp_send[2 * t + 1] = other.astype(BF16)

    pl.semaphore_wait(barrier, len(peers))

    def mp_copy(k):
        return remote(
            mp_send.at[lax.rem(mp + k, n_mp)], mp_recv.at[k - 1], mp_ss.at[k - 1], mp_rs.at[k - 1], mp_peer(k)
        )

    for k in far_first(n_mp):
        mp_copy(k).start()
    total = mp_send[mp].astype(F32)
    for k in reversed(far_first(n_mp)):
        mp_copy(k).wait_recv()
        total = total + mp_recv[k - 1].astype(F32)
    projected = total.astype(BF16).astype(F32)
    stacked = jnp.concatenate(
        [projected, pltpu.roll(projected, 64, 1), jnp.zeros((256 - tokens, 128), F32)], axis=0
    )
    rows_t[...] = stacked.T[:OWN, :].astype(BF16)

    loads[0].wait()
    y_lhs = rows_t[:32, :tokens]
    z_lhs = rows_t[32:, :tokens]
    width = side * OWN

    def z_blocks(offset):
        to_z = lax.rem(z + offset, side)
        for to_x in range(2):
            start = pl.multiple_of((to_x * side + to_z) * width, 128)
            grad = jnp.dot(z_lhs, act[:, pl.ds(start, width)], preferred_element_type=F32)
            for pair in range(side // 2):
                tile = grad[:, pair * 128 : (pair + 1) * 128]
                for lo, block in enumerate(halves(tile[:HALF], tile[HALF:], low_lanes(HALF))):
                    z_send[to_z, to_x, 2 * pair + lo] = block.astype(BF16)

    def y_blocks(offset):
        pair = lax.rem(y // 2 + offset, side // 2)
        for to_x in range(2):
            for q in range(side // 2):
                tiles = []
                for to_z in (2 * q, 2 * q + 1):
                    start = pl.multiple_of((to_x * side + to_z) * width + pair * 128, 128)
                    tiles.append(act[:, pl.ds(start, 128)])
                grad = jnp.dot(y_lhs, jnp.concatenate(tiles, axis=1), preferred_element_type=F32)
                for r in range(2):
                    tile = grad[:, r * 128 : (r + 1) * 128]
                    for lo, block in enumerate(halves(tile[:HALF], tile[HALF:], low_lanes(HALF))):
                        y_send[2 * pair + lo, to_x, 2 * q + r] = block.astype(BF16)

    def axis(pos, peer, send, recv1, recv2, recv3, recv4, ss, rs):
        def block(offset):
            return send.at[lax.rem(pos + offset, side)]

        up, down = (1, 2, 3), (side - 1, side - 2, side - 3)
        near, merged, far, across = [], [], [], []
        for way, (one, two, three) in enumerate((up, down)):
            near.append(remote(block(one), recv1.at[way], ss.at[0, way], rs.at[0, way], peer(one)))
            merged.append(remote(block(two), recv2.at[way], ss.at[1, way], rs.at[1, way], peer(two)))
            far.append(remote(block(three), recv3.at[way], ss.at[2, way], rs.at[2, way], peer(one)))
            across.append(remote(block(4).at[way], recv4.at[way], ss.at[3, way], rs.at[3, way], peer(two)))

        def merge():
            for way, two in enumerate((2, side - 2)):
                slot = lax.rem(pos + two, side)
                far[way].wait_recv()
                across[way].wait_recv()
                for to_x in range(2):
                    acc = send[slot, to_x].astype(F32) + recv3[way, to_x].astype(F32)
                    if to_x == way:
                        acc = acc + recv4[way].astype(F32)
                    send[slot, to_x] = acc.astype(BF16)
                merged[way].start()

        def total(out):
            for way in range(2):
                near[way].wait_recv()
                merged[way].wait_recv()
            for to_x in range(2):
                acc = send[pos, to_x].astype(F32)
                for recv in (recv1, recv2):
                    for way in range(2):
                        acc = acc + recv[way, to_x].astype(F32)
                acc = acc.astype(BF16)
                for q in range(side):
                    out[q, to_x] = acc[q]

        return near, merged, far, across, merge, total

    z_near, z_merged, z_far, z_across, z_merge, z_total = axis(
        z, z_peer, z_send, z_recv1, z_recv2, z_recv3, z_recv4, z_ss, z_rs
    )
    y_near, y_merged, y_far, y_across, y_merge, y_total = axis(
        y, y_peer, y_send, y_recv1, y_recv2, y_recv3, y_recv4, y_ss, y_rs
    )

    def begin(copies):
        for copy in copies:
            copy.start()

    z_blocks(4)
    begin(z_across)
    z_blocks(3)
    z_blocks(side - 3)
    begin(z_far)
    y_blocks(2)
    begin(y_across)
    y_blocks(1)
    y_blocks(3)
    begin(y_far)
    z_blocks(1)
    z_blocks(side - 1)
    begin(z_near)
    y_blocks(0)
    begin(y_near)
    z_blocks(2)
    z_blocks(side - 2)
    z_merge()
    y_merge()
    z_blocks(0)

    targets = [(k, flip) for k in far_first(side) for flip in (1, 0)] + [(0, 1)]

    def second_copies(pos, peer, send, recv, ss, rs):
        return [
            remote(
                send.at[lax.rem(pos + k, side), x + flip * (1 - 2 * x)],
                recv.at[i], ss.at[i], rs.at[i], peer(k, flip),
            )
            for i, (k, flip) in enumerate(targets)
        ]

    yy_copies = second_copies(y, xy_peer, yy_send, yy_recv, yy_ss, yy_rs)
    zz_copies = second_copies(z, xz_peer, zz_send, zz_recv, zz_ss, zz_rs)
    z_total(yy_send)
    begin(yy_copies)
    y_total(zz_send)
    begin(zz_copies)

    def add_second(copies, send, recv, own):
        acc = send[own, x].astype(F32)
        for i in reversed(range(len(copies))):
            copies[i].wait_recv()
            acc = acc + recv[i].astype(F32)
        return acc

    z_half = add_second(yy_copies, yy_send, yy_recv, y)
    y_half = add_second(zz_copies, zz_send, zz_recv, z)
    grad_t = jnp.concatenate([y_half, pltpu.roll(y_half, 64, 1), z_half, pltpu.roll(z_half, 64, 1)], axis=0)
    grad = grad_t.T[:OWN, :]

    loads[1].wait()
    loads[2].wait()
    moment_new = beta_first * moment[...] + (1.0 - beta_first) * grad
    second_new = beta_second * second[...] + (1.0 - beta_second) * grad * grad
    new_moment[...] = moment_new
    new_second[...] = second_new
    direction = moment_new / (jnp.sqrt(second_new) + epsilon)
    gather[mp] = jnp.concatenate([direction[:32], direction[32:]], axis=1).astype(BF16)

    def g_copy(k):
        return remote(gather.at[mp], gather.at[mp], g_ss.at[k - 1], g_rs.at[k - 1], mp_peer(k))

    for k in far_first(n_mp):
        g_copy(k).start()
    stores = [
        pltpu.make_async_copy(new_moment, moment_out, store_sem.at[0]),
        pltpu.make_async_copy(new_second, second_out, store_sem.at[1]),
    ]
    begin(stores)
    for k in range(1, n_mp):
        mp_copy(k).wait_send()
    for copies in (z_near, z_merged, z_far, z_across, y_near, y_merged, y_far, y_across, yy_copies, zz_copies):
        for copy in copies:
            copy.wait_send()
    loads[3].wait()

    def pair_of(steps):
        return lax.rem(mp // 2 + steps, n_mp // 2)

    def pair_tile(pair):
        top, bottom = halves(gather[2 * pair].astype(F32), gather[2 * pair + 1].astype(F32), low_lanes(32))
        return jnp.concatenate([top, bottom], axis=0).astype(BF16)

    def arrivals(pairs):
        for steps in pairs:
            for core in range(2):
                slot = 2 * pair_of(steps) + core
                k = lax.rem(mp + n_mp - slot, n_mp)

                @pl.when(k > 0)
                def _():
                    remote(gather.at[slot], gather.at[slot], g_ss.at[0], g_rs.at[k - 1], mp_peer(1)).wait_recv()

    pairs = n_mp // 2
    near_pairs, far_pairs = (0, 1), (pairs - 1, pairs - 2)
    for stage, group in enumerate((near_pairs, far_pairs)):
        arrivals(group)
        left = jnp.concatenate([pair_tile(pair_of(steps)) for steps in group], axis=1)
        columns = [pl.ds(pl.multiple_of(pair_of(steps) * 128, 128), 128) for steps in group]
        for i in range(parts):
            span = slice(i * DEPTH, (i + 1) * DEPTH)
            right = jnp.concatenate([basis[span, cols] for cols in columns], axis=1)
            update = lax.dot_general(left, right, (((1,), (1,)), ((), ())), preferred_element_type=F32)
            if stage == 0:
                half_weight[:, span] = weight[:, span].astype(F32) - step_size * update
            else:
                new_weight[:, span] = (half_weight[:, span] - step_size * update).astype(BF16)
                stores.append(pltpu.make_async_copy(new_weight.at[:, span], weight_out.at[:, span], store_sem.at[2 + i]))
                stores[-1].start()
    for k in range(1, n_mp):
        g_copy(k).wait_send()
    for copy in stores:
        copy.wait()


def copy_kernel(weight_in, moment_in, second_in, weight_out, moment_out, second_out, weight, moment, second, load_sem, store_sem):
    rows = [pl.ds(start, HALF) for start in range(0, OWN, HALF)]
    pieces = [(weight_in.at[r], weight.at[r], weight_out.at[r]) for r in rows]
    pieces += [(moment_in, moment, moment_out), (second_in, second, second_out)]
    loads = [pltpu.make_async_copy(a, b, load_sem.at[i]) for i, (a, b, _) in enumerate(pieces)]
    stores = [pltpu.make_async_copy(b, c, store_sem.at[i]) for i, (_, b, c) in enumerate(pieces)]
    for copy in loads:
        copy.start()
    for load, store in zip(loads, stores):
        load.wait()
        store.start()
    for copy in stores:
        copy.wait()


def shards(side, n_mp, activations, cotangent, subspace_basis, weight, moment, second):
    micro, tokens, width = activations.shape
    act = activations.reshape(micro * tokens, width)
    cot = cotangent.reshape(micro * tokens, cotangent.shape[2])
    units, rank = subspace_basis.shape
    dma = pltpu.SemaphoreType.DMA
    m = n_mp - 1
    n2 = 2 * side - 1
    plane = (side, HALF, 128)
    axis_recv = [
        pltpu.VMEM((2, 2) + plane, BF16),
        pltpu.VMEM((2, 2) + plane, BF16),
        pltpu.VMEM((2, 2) + plane, BF16),
        pltpu.VMEM((2,) + plane, BF16),
    ]
    scratch = [
        pltpu.VMEM(act.shape, BF16),
        pltpu.VMEM(cot.shape, BF16),
        pltpu.VMEM(subspace_basis.shape, BF16),
        pltpu.VMEM(weight.shape, BF16),
        pltpu.VMEM(moment.shape, F32),
        pltpu.VMEM(second.shape, F32),
        pltpu.VMEM(weight.shape, F32),
        pltpu.VMEM(weight.shape, BF16),
        pltpu.VMEM(moment.shape, F32),
        pltpu.VMEM(second.shape, F32),
        pltpu.VMEM((micro * tokens, rank), F32),
        pltpu.VMEM((n_mp, tokens, 128), BF16),
        pltpu.VMEM((m, tokens, 128), BF16),
        pltpu.VMEM((OWN, 256), BF16),
        pltpu.VMEM((side, 2) + plane, BF16),
        pltpu.VMEM((side, 2) + plane, BF16),
        *axis_recv,
        *axis_recv,
        pltpu.VMEM((side, 2, HALF, 128), BF16),
        pltpu.VMEM((side, 2, HALF, 128), BF16),
        pltpu.VMEM((n2, HALF, 128), BF16),
        pltpu.VMEM((n2, HALF, 128), BF16),
        pltpu.VMEM((n_mp, 32, 128), BF16),
        dma((4,)),
        dma((2, units // DEPTH)),
        dma((2 + units // DEPTH,)),
        dma((m,)), dma((m,)),
        dma((4, 2)), dma((4, 2)), dma((4, 2)), dma((4, 2)),
        dma((n2,)), dma((n2,)), dma((n2,)), dma((n2,)),
        dma((m,)), dma((m,)),
    ]
    hbm = pl.BlockSpec(memory_space=pltpu.HBM)
    shapes = tuple(jax.ShapeDtypeStruct(a.shape, a.dtype) for a in (weight, moment, second))
    results = pl.pallas_call(
        functools.partial(step_kernel, side, n_mp),
        out_shape=shapes,
        in_specs=[hbm] * 6,
        out_specs=(hbm,) * 3,
        scratch_shapes=scratch,
        compiler_params=pltpu.CompilerParams(
            collective_id=0, has_side_effects=True, vmem_limit_bytes=VMEM
        ),
    )(act, cot, subspace_basis, weight, moment, second)
    return pl.pallas_call(
        copy_kernel,
        out_shape=shapes,
        in_specs=[hbm] * 3,
        out_specs=(hbm,) * 3,
        scratch_shapes=[pltpu.VMEM(a.shape, a.dtype) for a in shapes]
        + [dma((2 + OWN // HALF,)), dma((2 + OWN // HALF,))],
        compiler_params=pltpu.CompilerParams(vmem_limit_bytes=VMEM),
    )(*results)


def solution(mesh):
    side = math.isqrt(mesh.shape["dp"] // 2)
    n_mp = mesh.shape["mp"]
    in_specs = (
        P(None, "dp", None),
        P(None, "dp", "mp"),
        P("mp", None),
        P("dp", "mp"),
        P("dp", "mp"),
        P("dp", "mp"),
    )
    out_specs = (P("dp", "mp"), P("dp", "mp"), P("dp", "mp"))
    return jax.shard_map(
        functools.partial(shards, side, n_mp), mesh=mesh, in_specs=in_specs, out_specs=out_specs, check_vma=False
    )
```
